32 devices in a mesh: gx: 8 (over z, y), gy: 4 (over x, core).
Axes of the slice: x: 2, y: 2, z: 4, core: 2. Of those that a mesh axis runs over, the one named last changes fastest.
Arguments:
- object_field: float32 [2, 2048, 4096], P(None, 'gy', 'gx'), may hold values from -6 to 6
- probe_field: float32 [2, 256, 256], replicated, may hold values from -5 to 5
- measured: float32 [4, 8, 4, 256, 256], P('gy', 'gx'), may hold values from 0 to 2.5
- offsets: int32 [4, 8, 4, 2], P('gy', 'gx'), may hold values from 0 to 512
- counts: int32 [4, 8], P('gy', 'gx'), may hold values from 1 to 4
Outputs:
- updated_object: float32 [2, 2048, 4096], P(None, 'gy', 'gx')
The draws below stay inside these ranges and needn't reach their ends.
Inputs may be any that keep to these rules, and one draw needn't show every extreme that they name: `offsets`: A window lies within its tile and the 128 cells around it. Windows 0 to counts - 1 of a tile are live, the others unused.
All inputs are finite; a program needn't handle non-finite values.
Results may differ from the reference program's by a relative error of at most 0.0055.
Values sent between devices are 32-bit elements; how exact they have to be, the bound alone decides.
A program may use at most 128 MiB of HBM per device.

```python
import math
import jax
import jax.numpy as jnp
from jax import lax

P_SIZE = 256
TILE = 512
WIN = 4
ITERS = 2
MARGIN = 128
NROWS = 2048
NCOLS = 4096
N_GX = 8
N_GY = 4


def plant(drawn, key, least, high):
    place = [jax.random.randint(jax.random.fold_in(key, axis), (), 0, length) for axis, length in enumerate(drawn.shape)]
    widest = drawn.shape.index(max(drawn.shape))
    beside = place[:widest] + [(place[widest] + 1) % drawn.shape[widest]] + place[widest + 1:]
    return drawn.at[tuple(place)].set(least).at[tuple(beside)].set(high)


def level_of(own_key, shape, cuts, low, high):
    gain = 1.0
    for dim, parts in cuts:
        draws = jax.random.uniform(jax.random.fold_in(jax.random.fold_in(own_key, 6), dim), (parts,), jnp.float32, low / len(cuts), high / len(cuts))
        gain = gain * jnp.repeat(jnp.exp(draws), shape[dim] // parts).reshape((-1,) + (1,) * (len(shape) - 1 - dim))
    return gain


def gaussian(own_key, dims, spread, bound, cuts=(), kind=jnp.bfloat16):
    values = jax.random.normal(own_key, dims, jnp.float32) * spread
    if len(cuts) > 0:
        values = level_of(own_key, dims, cuts, -0.22, 0.18) * values
    return jnp.clip(values, min=-bound, max=bound).astype(kind)


def setup_inputs(seed: int = 0) -> dict:
    key_of = jax.random.split(jax.random.key(seed), 6)
    object_field = gaussian(key_of[0], (2, NROWS, NCOLS), 1.0, 6.0, ((1, 4), (2, 8)), jnp.float32)
    probe_field = gaussian(key_of[1], (2, P_SIZE, P_SIZE), 1.0, 5.0, (), jnp.float32)
    measured = jnp.clip(2.5 * jax.random.uniform(key_of[2], (N_GY, N_GX, WIN, P_SIZE, P_SIZE), jnp.float32) ** level_of(key_of[2], (N_GY, N_GX, WIN, P_SIZE, P_SIZE), ((0, 4), (1, 8)), -0.2, 0.2), 0.0, 2.5)
    offsets = plant(jax.random.randint(key_of[3], (N_GY, N_GX, WIN, 2), 0, TILE + 1), jax.random.fold_in(key_of[3], 1), 0, TILE).astype(jnp.int32)
    counts = plant(jax.random.randint(key_of[4], (N_GY, N_GX), 1, WIN + 1), jax.random.fold_in(key_of[4], 1), 1, WIN).astype(jnp.int32)
    return dict(object_field=object_field, probe_field=probe_field, measured=measured, offsets=offsets, counts=counts)


step_size = 0.25
amplitude_floor = 0.5

def tables(window_side):
    indices = jnp.arange(window_side, dtype=jnp.int32)
    phases = (indices[:, None] * indices[None, :] % window_side).astype(jnp.float32) * (2.0 * math.pi / window_side)
    norm_scale = 1.0 / math.sqrt(window_side)
    return ((jnp.cos(phases) * norm_scale).astype(jnp.bfloat16), (jnp.sin(phases) * norm_scale).astype(jnp.bfloat16))

def left_product(matrix, stacked):
    return jnp.einsum('ik,wkj->wij', matrix.astype(jnp.float32), stacked.astype(jnp.float32))

def right_product(stacked, matrix):
    return jnp.einsum('wik,kj->wij', stacked.astype(jnp.float32), matrix.astype(jnp.float32))

def transform(real_part, imag_part, cosine_table, sines_signed):
    half_real = (left_product(cosine_table, real_part) - left_product(sines_signed, imag_part)).astype(jnp.bfloat16)
    half_imag = (left_product(cosine_table, imag_part) + left_product(sines_signed, real_part)).astype(jnp.bfloat16)
    far_real = right_product(half_real, cosine_table) - right_product(half_imag, sines_signed)
    far_imag = right_product(half_real, sines_signed) + right_product(half_imag, cosine_table)
    return (far_real, far_imag)

def window_gradient(patches, probe_field, amplitudes, cosine_table, sine_table):
    probe_real, probe_imag = (probe_field[0], probe_field[1])
    patch_real, patch_imag = (patches[:, 0], patches[:, 1])
    exit_real = (probe_real * patch_real - probe_imag * patch_imag).astype(jnp.bfloat16)
    exit_imag = (probe_real * patch_imag + probe_imag * patch_real).astype(jnp.bfloat16)
    far_real, far_imag = transform(exit_real, exit_imag, cosine_table, -sine_table)
    modulus = jnp.sqrt(far_real * far_real + far_imag * far_imag)
    factor = 1.0 - amplitudes / jnp.maximum(modulus, amplitude_floor)
    back_real, back_imag = transform((far_real * factor).astype(jnp.bfloat16), (far_imag * factor).astype(jnp.bfloat16), cosine_table, sine_table)
    return jnp.stack((probe_real * back_real + probe_imag * back_imag, probe_real * back_imag - probe_imag * back_real), axis=1)

def reference(object_field, probe_field, measured, offsets, counts):
    cosine_table, sine_table = tables(P_SIZE)
    amplitudes = measured.reshape(N_GY * N_GX, WIN, P_SIZE, P_SIZE)
    starts = offsets.reshape(N_GY * N_GX, WIN, 2)
    live_counts = counts.reshape(N_GY * N_GX)
    for iteration in range(ITERS):
        padded = jnp.pad(object_field, ((0, 0), (MARGIN, MARGIN), (MARGIN, MARGIN)))

        def tile_step(gradient, tile_index):
            tile_row = tile_index // N_GX * TILE
            tile_col = tile_index % N_GX * TILE
            corner = starts[tile_index]
            patches = jax.vmap(lambda window_start: lax.dynamic_slice(padded, (jnp.int32(0), tile_row + window_start[0], tile_col + window_start[1]), (2, P_SIZE, P_SIZE)))(corner)
            live_mask = (jnp.arange(WIN, dtype=jnp.int32) < live_counts[tile_index]).astype(jnp.float32)
            contributions = window_gradient(patches, probe_field, amplitudes[tile_index], cosine_table, sine_table) * live_mask[:, None, None, None]

            def deposit(window, total):
                row_start = tile_row + corner[window, 0]
                col_start = tile_col + corner[window, 1]
                current = lax.dynamic_slice(total, (jnp.int32(0), row_start, col_start), (2, P_SIZE, P_SIZE))
                return lax.dynamic_update_slice(total, current + contributions[window], (jnp.int32(0), row_start, col_start))
            return (lax.fori_loop(0, WIN, deposit, gradient), None)
        gradient, _ = lax.scan(tile_step, jnp.zeros_like(padded), jnp.arange(N_GY * N_GX, dtype=jnp.int32))
        object_field = object_field - step_size * gradient[:, MARGIN:MARGIN + NROWS, MARGIN:MARGIN + NCOLS]
    return object_field
```

```python
import functools
import math

import jax
import jax.numpy as jnp
import ml_dtypes
import numpy as np
from jax import lax
from jax.experimental import pallas as pl
from jax.experimental.pallas import tpu as pltpu
from jax.sharding import PartitionSpec as P

ITERS = 2
STEP = 0.25
FLOOR = 0.5
LANES = 128
SUBLANES = 8
VMEM_LIMIT = 40 * 1024 * 1024
MESH = pl.DeviceIdType.MESH
VM = pl.BlockSpec(memory_space=pltpu.VMEM)
SM = pl.BlockSpec(memory_space=pltpu.SMEM)


def tables(side):
    indices = np.arange(side)
    phases = (indices[:, None] * indices[None, :] % side) * (2.0 * math.pi / side)
    scale = 1.0 / math.sqrt(side)
    return (
        (np.cos(phases) * scale).astype(ml_dtypes.bfloat16),
        (np.sin(phases) * scale).astype(ml_dtypes.bfloat16),
    )


def dot(a, b):
    return jnp.dot(a, b, preferred_element_type=jnp.float32)


def window_kernel(ext_ref, probe_ref, amp_ref, cos_ref, sin_ref, starts_ref, counts_ref, grad_ref):
    side = probe_ref.shape[1]
    wide = side + LANES
    tall = side + SUBLANES
    last_base = (ext_ref.shape[2] - wide) // LANES
    last_row_base = (ext_ref.shape[1] - tall) // SUBLANES

    def clear(i, carry):
        rows = pl.ds(pl.multiple_of(i * 8, 8), 8)
        grad_ref[:, rows, :] = jnp.zeros((2, 8, grad_ref.shape[2]), jnp.float32)
        return carry

    lax.fori_loop(0, grad_ref.shape[1] // 8, clear, 0)

    def window(w, carry):
        row = starts_ref[w, 0]
        col = starts_ref[w, 1]
        base = jnp.minimum(col // LANES, last_base) * LANES
        shift = col - base
        row_base = jnp.minimum(row // SUBLANES, last_row_base) * SUBLANES
        row_shift = row - row_base
        rows = pl.ds(pl.multiple_of(row_base, SUBLANES), tall)
        back_row_shift = jnp.where(row_shift == 0, 0, tall - row_shift)
        cols = pl.ds(pl.multiple_of(base, LANES), wide)
        back_shift = jnp.where(shift == 0, 0, wide - shift)

        def patch(k):
            block = pltpu.roll(ext_ref[k, rows, cols], back_shift, axis=1)[:, :side]
            return pltpu.roll(block, back_row_shift, axis=0)[:side]

        pr, pi = probe_ref[0], probe_ref[1]
        qr, qi = patch(0), patch(1)
        er = (pr * qr - pi * qi).astype(jnp.bfloat16)
        ei = (pr * qi + pi * qr).astype(jnp.bfloat16)
        ct, st = cos_ref[...], sin_ref[...]
        hr = (dot(ct, er) + dot(st, ei)).astype(jnp.bfloat16)
        hi = (dot(ct, ei) - dot(st, er)).astype(jnp.bfloat16)
        fr = dot(hr, ct) + dot(hi, st)
        fi = dot(hi, ct) - dot(hr, st)
        factor = 1.0 - amp_ref[w] * lax.rsqrt(jnp.maximum(fr * fr + fi * fi, FLOOR * FLOOR))
        xr = (fr * factor).astype(jnp.bfloat16)
        xi = (fi * factor).astype(jnp.bfloat16)
        gr = (dot(ct, xr) - dot(st, xi)).astype(jnp.bfloat16)
        gi = (dot(ct, xi) + dot(st, xr)).astype(jnp.bfloat16)
        br = dot(gr, ct) - dot(gi, st)
        bi = dot(gr, st) + dot(gi, ct)
        below = jnp.zeros((SUBLANES, side), jnp.float32)
        beside = jnp.zeros((tall, LANES), jnp.float32)

        def deposit(k, value):
            placed = pltpu.roll(jnp.concatenate([value, below], axis=0), row_shift, axis=0)
            placed = pltpu.roll(jnp.concatenate([placed, beside], axis=1), shift, axis=1)
            grad_ref[k, rows, cols] += placed

        deposit(0, pr * br + pi * bi)
        deposit(1, pr * bi - pi * br)
        return carry

    lax.fori_loop(0, counts_ref[0, 0], window, 0)


def window_call(ext, probe, amps, cos, sin, starts, counts):
    return pl.pallas_call(
        window_kernel,
        out_shape=jax.ShapeDtypeStruct(ext.shape, jnp.float32),
        in_specs=[VM] * 5 + [SM] * 2,
        out_specs=VM,
        compiler_params=pltpu.CompilerParams(vmem_limit_bytes=VMEM_LIMIT),
    )(ext, probe, amps, cos, sin, starts, counts)


class Place:
    def __init__(self):
        self.gx, self.gy = lax.axis_index("gx"), lax.axis_index("gy")
        nx, ny = lax.axis_size("gx"), lax.axis_size("gy")
        self.has_x = (self.gx > 0, self.gx < nx - 1)
        self.has_y = (self.gy > 0, self.gy < ny - 1)
        self.to_x = ({"gx": self.gx - 1}, {"gx": self.gx + 1})
        self.to_y = ({"gy": self.gy - 1}, {"gy": self.gy + 1})

    def barrier(self):
        sem = pltpu.get_barrier_semaphore()
        pairs = list(zip(self.has_x + self.has_y, self.to_x + self.to_y))
        for has, to in pairs:

            @pl.when(has)
            def _():
                pl.semaphore_signal(sem, inc=1, device_id=to, device_id_type=MESH)

        peers = sum(has.astype(jnp.int32) for has, _ in pairs)
        pl.semaphore_wait(sem, peers)


def remote(src, dst, sems, index, to):
    return pltpu.make_async_remote_copy(
        src_ref=src,
        dst_ref=dst,
        send_sem=sems[0].at[index],
        recv_sem=sems[1].at[index],
        device_id=to,
        device_id_type=MESH,
    )


def by_rows(first, count, body, step=8):
    def one(i, carry):
        body(pl.multiple_of(first + i * step, 8))
        return carry

    lax.fori_loop(0, count // step, one, 0)


def halo_kernel(m, obj_ref, ext_ref, xs, xr, ys, yr):
    t = obj_ref.shape[1]
    place = Place()
    place.barrier()
    row_chunks = ((0, m), (t - m, m), (m, t - 2 * m))

    def x_copy(side, chunk):
        first, count = row_chunks[chunk]
        src_col = 0 if side == 0 else t - m
        dst_col = m + t if side == 0 else 0
        return remote(
            obj_ref.at[:, pl.ds(first, count), pl.ds(src_col, m)],
            ext_ref.at[:, pl.ds(m + first, count), pl.ds(dst_col, m)],
            (xs, xr),
            (side, chunk),
            place.to_x[side],
        )

    def y_copy(side, part):
        src_row = 0 if side == 0 else t - m
        dst_row = m + t if side == 0 else 0
        if part == 0:
            src = obj_ref.at[:, pl.ds(src_row, m), :]
            cols = pl.ds(m, t)
        else:
            cols = pl.ds(0 if part == 1 else m + t, m)
            src = ext_ref.at[:, pl.ds(m + src_row, m), cols]
        return remote(src, ext_ref.at[:, pl.ds(dst_row, m), cols], (ys, yr), (side, part), place.to_y[side])

    for chunk in range(3):
        for side in range(2):

            @pl.when(place.has_x[side])
            def _():
                x_copy(side, chunk).start()

    for side in range(2):

        @pl.when(place.has_y[side])
        def _():
            y_copy(side, 0).start()

    def centre(row):
        ext_ref[:, pl.ds(pl.multiple_of(row + m, 8), 8), m : m + t] = obj_ref[:, pl.ds(row, 8), :]

    by_rows(0, t, centre)
    for side in range(2):
        edge = 0 if side == 0 else m + t

        @pl.when(jnp.logical_not(place.has_x[side]))
        def _():
            def blank(row):
                ext_ref[:, pl.ds(row, 8), edge : edge + m] = jnp.zeros((2, 8, m), jnp.float32)

            by_rows(m, t, blank)

        @pl.when(jnp.logical_not(place.has_y[side]))
        def _():
            def blank(row):
                ext_ref[:, pl.ds(row, 8), :] = jnp.zeros((2, 8, t + 2 * m), jnp.float32)

            by_rows(edge, m, blank)

    for chunk in range(2):
        for side in range(2):

            @pl.when(place.has_x[side])
            def _():
                x_copy(1 - side, chunk).wait_recv()

        @pl.when(place.has_y[chunk])
        def _():
            y_copy(chunk, 1).start()
            y_copy(chunk, 2).start()

    for side in range(2):

        @pl.when(place.has_x[side])
        def _():
            x_copy(1 - side, 2).wait_recv()
            for chunk in range(3):
                x_copy(side, chunk).wait_send()

        @pl.when(place.has_y[side])
        def _():
            for part in range(3):
                y_copy(1 - side, part).wait_recv()
                y_copy(side, part).wait_send()


def sum_kernel(m, last, grad_ref, ext_ref, out_ref, ybuf, xbuf, xs, xr, ys, yr, hs, hr):
    full = ext_ref.shape[1]
    t = full - 2 * m
    w = m if last else 2 * m
    place = Place()
    place.barrier()
    top, bottom = (m, m), (t, m)
    half = (t - 2 * m) // 2
    mid1, mid2 = (2 * m, half), (2 * m + half, half)
    row_chunks = (mid1, top, bottom, mid2)

    def y_copy(side):
        src_row = 0 if side == 0 else m + t
        return remote(
            grad_ref.at[:, pl.ds(src_row, m), :],
            ybuf.at[1 - side],
            (ys, yr),
            side,
            place.to_y[side],
        )

    def x_copy(side, chunk):
        first, count = row_chunks[chunk]
        col = 0 if side == 0 else full - w
        return remote(
            grad_ref.at[:, pl.ds(first, count), pl.ds(col, w)],
            xbuf.at[1 - side, :, pl.ds(first - m, count), :],
            (xs, xr),
            (side, chunk),
            place.to_x[side],
        )

    def x_send(chunk):
        for side in range(2):

            @pl.when(place.has_x[side])
            def _():
                x_copy(side, chunk).start()

    for side in range(2):

        @pl.when(place.has_y[side])
        def _():
            y_copy(side).start()

    x_send(0)
    if last:
        x_send(3)
    for side in range(2):
        first = m if side == 0 else t

        @pl.when(place.has_y[side])
        def _():
            y_copy(1 - side).wait_recv()

            def add(row):
                grad_ref[:, pl.ds(row, 8), :] += ybuf[side, :, pl.ds(pl.multiple_of(row - first, 8), 8), :]

            by_rows(first, m, add)

        x_send(1 + side)
    if not last:
        x_send(3)

    def update(chunk):
        first, count = row_chunks[chunk]
        for side in range(2):

            @pl.when(place.has_x[side])
            def _():
                x_copy(1 - side, chunk).wait_recv()
                x_copy(side, chunk).wait_send()

                col = 2 * m - w if side == 0 else t

                def add(row):
                    piece = xbuf[side, :, pl.ds(pl.multiple_of(row - m, 8), 8), :]
                    grad_ref[:, pl.ds(row, 8), col : col + w] += piece

                by_rows(first, count, add)

        def step(row):
            rows = pl.ds(row, 8)
            if last:
                out_rows = pl.ds(pl.multiple_of(row - m, 8), 8)
                out_ref[:, out_rows, :] = ext_ref[:, rows, m : m + t] - STEP * grad_ref[:, rows, m : m + t]
            else:
                out_ref[:, rows, :] = ext_ref[:, rows, :] - STEP * grad_ref[:, rows, :]

        by_rows(first, count, step)
        if not last:
            for side in range(2):
                edge = 0 if side == 0 else m + t

                @pl.when(jnp.logical_not(place.has_x[side]))
                def _():
                    def blank(row):
                        out_ref[:, pl.ds(row, 8), edge : edge + m] = jnp.zeros((2, 8, m), jnp.float32)

                    by_rows(first, count, blank)

    def h_copy(side):
        src_row = m if side == 0 else t
        dst_row = m + t if side == 0 else 0
        return remote(
            out_ref.at[:, pl.ds(src_row, m), :],
            out_ref.at[:, pl.ds(dst_row, m), :],
            (hs, hr),
            side,
            place.to_y[side],
        )

    if last:
        for chunk in (0, 3, 1, 2):
            update(chunk)
    else:
        update(0)
        for side in range(2):
            update(1 + side)

            @pl.when(place.has_y[side])
            def _():
                h_copy(side).start()

        update(3)
    for side in range(2):

        @pl.when(place.has_y[side])
        def _():
            y_copy(side).wait_send()
            if not last:
                h_copy(1 - side).wait_recv()
                h_copy(side).wait_send()

        if not last:
            edge = 0 if side == 0 else m + t

            @pl.when(jnp.logical_not(place.has_y[side]))
            def _():
                def blank(row):
                    out_ref[:, pl.ds(row, 8), :] = jnp.zeros((2, 8, full), jnp.float32)

                by_rows(edge, m, blank)


def params(collective_id):
    return pltpu.CompilerParams(
        collective_id=collective_id, has_side_effects=True, vmem_limit_bytes=VMEM_LIMIT
    )


def halo_call(obj, m):
    t = obj.shape[1]
    full = t + 2 * m
    dma = pltpu.SemaphoreType.DMA
    return pl.pallas_call(
        functools.partial(halo_kernel, m),
        out_shape=jax.ShapeDtypeStruct((2, full, full), jnp.float32),
        in_specs=[VM],
        out_specs=VM,
        scratch_shapes=[dma((2, 3))] * 4,
        compiler_params=params(0),
    )(obj)


def sum_call(grad, ext, m, last, collective_id):
    full = ext.shape[1]
    t = full - 2 * m
    w = m if last else 2 * m
    side = t if last else full
    dma = pltpu.SemaphoreType.DMA
    return pl.pallas_call(
        functools.partial(sum_kernel_entry, m, last),
        out_shape=jax.ShapeDtypeStruct((2, side, side), jnp.float32),
        in_specs=[VM, VM],
        out_specs=VM,
        scratch_shapes=[
            pltpu.VMEM((2, full, full), jnp.float32),
            pltpu.VMEM((2, 2, m, full), jnp.float32),
            pltpu.VMEM((2, 2, t, w), jnp.float32),
            dma((2, 4)),
            dma((2, 4)),
            dma((2,)),
            dma((2,)),
            dma((2,)),
            dma((2,)),
        ],
        compiler_params=params(collective_id),
    )(grad, ext)


def sum_kernel_entry(m, last, grad_in, ext_ref, out_ref, work, *rest):
    def copy(row):
        work[:, pl.ds(row, 8), :] = grad_in[:, pl.ds(row, 8), :]

    by_rows(0, work.shape[1], copy)
    sum_kernel(m, last, work, ext_ref, out_ref, *rest)


def local(object_field, probe_field, measured, offsets, counts):
    side = probe_field.shape[1]
    m = side // 2
    cos, sin = tables(side)
    amps, starts = measured[0, 0], offsets[0, 0]
    ext = halo_call(object_field, m)
    for iteration in range(ITERS):
        last = iteration + 1 == ITERS
        grad = window_call(ext, probe_field, amps, cos, sin, starts, counts)
        ext = sum_call(grad, ext, m, last, 1 + iteration)
    return ext


def solution(mesh):
    return jax.shard_map(
        local,
        mesh=mesh,
        in_specs=(
            P(None, "gy", "gx"),
            P(),
            P("gy", "gx", None, None, None),
            P("gy", "gx", None, None),
            P("gy", "gx"),
        ),
        out_specs=P(None, "gy", "gx"),
        check_vma=False,
    )
```

```python
import functools
import math

import jax
import jax.numpy as jnp
import ml_dtypes
import numpy as np
from jax import lax
from jax.experimental import pallas as pl
from jax.experimental.pallas import tpu as pltpu
from jax.sharding import PartitionSpec as P

ITERS = 2
STEP = 0.25
FLOOR = 0.5
LANES = 128
SUBLANES = 8
GROUP = 2
VMEM_LIMIT = 40 * 1024 * 1024
MESH = pl.DeviceIdType.MESH
VM = pl.BlockSpec(memory_space=pltpu.VMEM)
SM = pl.BlockSpec(memory_space=pltpu.SMEM)


def tables(side):
    indices = np.arange(side)
    phases = (indices[:, None] * indices[None, :] % side) * (2.0 * math.pi / side)
    scale = 1.0 / math.sqrt(side)
    cos = (np.cos(phases) * scale).astype(ml_dtypes.bfloat16)
    sin = (np.sin(phases) * scale).astype(ml_dtypes.bfloat16)
    return np.block([[cos, sin], [-sin, cos]]), np.block([[cos, -sin], [sin, cos]])


def dot(a, b):
    return jnp.dot(a, b, preferred_element_type=jnp.float32)


def shifted(block, amount, direction):
    bit = SUBLANES
    while bit > 0:
        turned = pltpu.roll(block, bit if direction > 0 else block.shape[0] - bit, axis=0)
        block = jnp.where(amount & bit != 0, turned, block)
        bit //= 2
    return block


def window_kernel(ext_ref, probe_ref, amp_ref, fore_ref, aft_ref, starts_ref, counts_ref, grad_ref):
    side = probe_ref.shape[1]
    windows = amp_ref.shape[0]
    wide = side + LANES
    tall = side + SUBLANES
    last_base = (ext_ref.shape[2] - wide) // LANES
    last_row_base = (ext_ref.shape[1] - tall) // SUBLANES
    count = counts_ref[0, 0]

    def clear(i, carry):
        rows = pl.ds(pl.multiple_of(i * 8, 8), 8)
        grad_ref[:, rows, :] = jnp.zeros((2, 8, grad_ref.shape[2]), jnp.float32)
        return carry

    lax.fori_loop(0, grad_ref.shape[1] // 8, clear, 0)

    def product(left, middle, right):
        half = dot(left, middle).astype(jnp.bfloat16)
        return dot(jnp.concatenate([half[:side], half[side:]], axis=1), right)

    def place(w):
        row = starts_ref[0, w]
        col = starts_ref[1, w]
        base = jnp.minimum(col // LANES, last_base) * LANES
        row_base = jnp.minimum(row // SUBLANES, last_row_base) * SUBLANES
        rows = pl.ds(pl.multiple_of(row_base, SUBLANES), tall)
        cols = pl.ds(pl.multiple_of(base, LANES), wide)
        return rows, cols, row - row_base, col - base

    def contribution(w):
        rows, cols, row_shift, shift = place(w)
        back_shift = jnp.where(shift == 0, 0, wide - shift)

        def patch(k):
            block = pltpu.roll(ext_ref[k, rows, cols], back_shift, axis=1)[:, :side]
            return shifted(block, row_shift, -1)[:side]

        pr, pi = probe_ref[0], probe_ref[1]
        qr, qi = patch(0), patch(1)
        exit_field = jnp.concatenate(
            [(pr * qr - pi * qi).astype(jnp.bfloat16), (pr * qi + pi * qr).astype(jnp.bfloat16)], axis=0
        )
        fore, aft = fore_ref[...], aft_ref[...]
        far = product(fore, exit_field, aft)
        fr, fi = far[:, :side], far[:, side:]
        factor = 1.0 - amp_ref[w] * lax.rsqrt(jnp.maximum(fr * fr + fi * fi, FLOOR * FLOOR))
        chi = jnp.concatenate(
            [(fr * factor).astype(jnp.bfloat16), (fi * factor).astype(jnp.bfloat16)], axis=0
        )
        back = product(aft, chi, fore)
        br, bi = back[:, :side], back[:, side:]
        return pr * br + pi * bi, pr * bi - pi * br

    def deposit(w, parts):
        rows, cols, row_shift, shift = place(w)
        below = jnp.zeros((SUBLANES, side), jnp.float32)
        beside = jnp.zeros((tall, LANES), jnp.float32)
        for k in range(2):
            placed = shifted(jnp.concatenate([parts[k], below], axis=0), row_shift, 1)
            placed = pltpu.roll(jnp.concatenate([placed, beside], axis=1), shift, axis=1)
            grad_ref[k, rows, cols] += placed

    for first in range(0, windows, GROUP):
        group = range(first, min(first + GROUP, windows))

        @pl.when(first < count)
        def _():
            parts = [contribution(w) for w in group]
            for w, part in zip(group, parts):
                if w == first:
                    deposit(w, part)
                else:

                    @pl.when(w < count)
                    def _():
                        deposit(w, part)


def window_call(ext, probe, amps, fore, aft, starts, counts):
    return pl.pallas_call(
        window_kernel,
        out_shape=jax.ShapeDtypeStruct(ext.shape, jnp.float32),
        in_specs=[VM] * 5 + [SM] * 2,
        out_specs=VM,
        compiler_params=pltpu.CompilerParams(vmem_limit_bytes=VMEM_LIMIT),
    )(ext, probe, amps, fore, aft, starts, counts)


class Place:
    def __init__(self):
        self.gx, self.gy = lax.axis_index("gx"), lax.axis_index("gy")
        nx, ny = lax.axis_size("gx"), lax.axis_size("gy")
        self.has_x = (self.gx > 0, self.gx < nx - 1)
        self.has_y = (self.gy > 0, self.gy < ny - 1)
        self.to_x = ({"gx": self.gx - 1}, {"gx": self.gx + 1})
        self.to_y = ({"gy": self.gy - 1}, {"gy": self.gy + 1})

    def barrier(self):
        sem = pltpu.get_barrier_semaphore()
        pairs = list(zip(self.has_x + self.has_y, self.to_x + self.to_y))
        for has, to in pairs:

            @pl.when(has)
            def _():
                pl.semaphore_signal(sem, inc=1, device_id=to, device_id_type=MESH)

        peers = sum(has.astype(jnp.int32) for has, _ in pairs)
        pl.semaphore_wait(sem, peers)


def remote(src, dst, sems, index, to):
    return pltpu.make_async_remote_copy(
        src_ref=src,
        dst_ref=dst,
        send_sem=sems[0].at[index],
        recv_sem=sems[1].at[index],
        device_id=to,
        device_id_type=MESH,
    )


def by_rows(first, count, body, step=8):
    def one(i, carry):
        body(pl.multiple_of(first + i * step, 8))
        return carry

    lax.fori_loop(0, count // step, one, 0)


def halo_kernel(m, obj_ref, ext_ref, xs, xr, ys, yr, own_sem):
    t = obj_ref.shape[1]
    place = Place()
    place.barrier()
    row_chunks = ((0, m), (t - m, m), (m, t - 2 * m))

    def x_copy(side, chunk):
        first, count = row_chunks[chunk]
        src_col = 0 if side == 0 else t - m
        dst_col = m + t if side == 0 else 0
        return remote(
            obj_ref.at[:, pl.ds(first, count), pl.ds(src_col, m)],
            ext_ref.at[:, pl.ds(m + first, count), pl.ds(dst_col, m)],
            (xs, xr),
            (side, chunk),
            place.to_x[side],
        )

    def y_copy(side, part):
        src_row = 0 if side == 0 else t - m
        dst_row = m + t if side == 0 else 0
        if part == 0:
            src = obj_ref.at[:, pl.ds(src_row, m), :]
            cols = pl.ds(m, t)
        else:
            cols = pl.ds(0 if part == 1 else m + t, m)
            src = ext_ref.at[:, pl.ds(m + src_row, m), cols]
        return remote(src, ext_ref.at[:, pl.ds(dst_row, m), cols], (ys, yr), (side, part), place.to_y[side])

    for chunk in range(3):
        for side in range(2):

            @pl.when(place.has_x[side])
            def _():
                x_copy(side, chunk).start()

    for side in range(2):

        @pl.when(place.has_y[side])
        def _():
            y_copy(side, 0).start()

    centre = pltpu.make_async_copy(obj_ref, ext_ref.at[:, pl.ds(m, t), pl.ds(m, t)], own_sem)
    centre.start()
    for side in range(2):
        edge = 0 if side == 0 else m + t

        @pl.when(jnp.logical_not(place.has_x[side]))
        def _():
            def blank(row):
                ext_ref[:, pl.ds(row, 8), edge : edge + m] = jnp.zeros((2, 8, m), jnp.float32)

            by_rows(m, t, blank)

        @pl.when(jnp.logical_not(place.has_y[side]))
        def _():
            def blank(row):
                ext_ref[:, pl.ds(row, 8), :] = jnp.zeros((2, 8, t + 2 * m), jnp.float32)

            by_rows(edge, m, blank)

    centre.wait()
    for chunk in range(2):
        for side in range(2):

            @pl.when(place.has_x[side])
            def _():
                x_copy(1 - side, chunk).wait_recv()

        @pl.when(place.has_y[chunk])
        def _():
            y_copy(chunk, 1).start()
            y_copy(chunk, 2).start()

    for side in range(2):

        @pl.when(place.has_x[side])
        def _():
            x_copy(1 - side, 2).wait_recv()
            for chunk in range(3):
                x_copy(side, chunk).wait_send()

        @pl.when(place.has_y[side])
        def _():
            for part in range(3):
                y_copy(1 - side, part).wait_recv()
                y_copy(side, part).wait_send()


def sum_kernel(m, last, grad_ref, ext_ref, out_ref, ybuf, xbuf, xs, xr, ys, yr, hs, hr):
    full = ext_ref.shape[1]
    t = full - 2 * m
    w = m if last else 2 * m
    place = Place()
    place.barrier()
    top, bottom = (m, m), (t, m)
    half = (t - 2 * m) // 2
    mid1, mid2 = (2 * m, half), (2 * m + half, half)
    row_chunks = (mid1, top, bottom, mid2)

    def y_copy(side):
        src_row = 0 if side == 0 else m + t
        return remote(
            grad_ref.at[:, pl.ds(src_row, m), :],
            ybuf.at[1 - side],
            (ys, yr),
            side,
            place.to_y[side],
        )

    def x_copy(side, chunk):
        first, count = row_chunks[chunk]
        col = 0 if side == 0 else full - w
        return remote(
            grad_ref.at[:, pl.ds(first, count), pl.ds(col, w)],
            xbuf.at[1 - side, :, pl.ds(first - m, count), :],
            (xs, xr),
            (side, chunk),
            place.to_x[side],
        )

    def x_send(chunk):
        for side in range(2):

            @pl.when(place.has_x[side])
            def _():
                x_copy(side, chunk).start()

    for side in range(2):

        @pl.when(place.has_y[side])
        def _():
            y_copy(side).start()

    x_send(0)
    if last:
        x_send(3)
    for side in range(2):
        first = m if side == 0 else t

        @pl.when(place.has_y[side])
        def _():
            y_copy(1 - side).wait_recv()

            def add(row):
                grad_ref[:, pl.ds(row, 8), :] += ybuf[side, :, pl.ds(pl.multiple_of(row - first, 8), 8), :]

            by_rows(first, m, add)

        x_send(1 + side)
    if not last:
        x_send(3)

    def update(chunk):
        first, count = row_chunks[chunk]
        for side in range(2):

            @pl.when(place.has_x[side])
            def _():
                x_copy(1 - side, chunk).wait_recv()
                x_copy(side, chunk).wait_send()

                col = 2 * m - w if side == 0 else t

                def add(row):
                    piece = xbuf[side, :, pl.ds(pl.multiple_of(row - m, 8), 8), :]
                    grad_ref[:, pl.ds(row, 8), col : col + w] += piece

                by_rows(first, count, add)

        def step(row):
            rows = pl.ds(row, 8)
            if last:
                out_rows = pl.ds(pl.multiple_of(row - m, 8), 8)
                out_ref[:, out_rows, :] = ext_ref[:, rows, m : m + t] - STEP * grad_ref[:, rows, m : m + t]
            else:
                out_ref[:, rows, :] = ext_ref[:, rows, :] - STEP * grad_ref[:, rows, :]

        by_rows(first, count, step)
        if not last:
            for side in range(2):
                edge = 0 if side == 0 else m + t

                @pl.when(jnp.logical_not(place.has_x[side]))
                def _():
                    def blank(row):
                        out_ref[:, pl.ds(row, 8), edge : edge + m] = jnp.zeros((2, 8, m), jnp.float32)

                    by_rows(first, count, blank)

    def h_copy(side):
        src_row = m if side == 0 else t
        dst_row = m + t if side == 0 else 0
        return remote(
            out_ref.at[:, pl.ds(src_row, m), :],
            out_ref.at[:, pl.ds(dst_row, m), :],
            (hs, hr),
            side,
            place.to_y[side],
        )

    if last:
        for chunk in (0, 3, 1, 2):
            update(chunk)
    else:
        update(0)
        for side in range(2):
            update(1 + side)

            @pl.when(place.has_y[side])
            def _():
                h_copy(side).start()

        update(3)
    for side in range(2):

        @pl.when(place.has_y[side])
        def _():
            y_copy(side).wait_send()
            if not last:
                h_copy(1 - side).wait_recv()
                h_copy(side).wait_send()

        if not last:
            edge = 0 if side == 0 else m + t

            @pl.when(jnp.logical_not(place.has_y[side]))
            def _():
                def blank(row):
                    out_ref[:, pl.ds(row, 8), :] = jnp.zeros((2, 8, full), jnp.float32)

                by_rows(edge, m, blank)


def params(collective_id):
    return pltpu.CompilerParams(
        collective_id=collective_id, has_side_effects=True, vmem_limit_bytes=VMEM_LIMIT
    )


def halo_call(obj, m):
    t = obj.shape[1]
    full = t + 2 * m
    dma = pltpu.SemaphoreType.DMA
    return pl.pallas_call(
        functools.partial(halo_kernel, m),
        out_shape=jax.ShapeDtypeStruct((2, full, full), jnp.float32),
        in_specs=[pl.BlockSpec(memory_space=pltpu.HBM)],
        out_specs=VM,
        scratch_shapes=[dma((2, 3))] * 4 + [dma],
        compiler_params=params(0),
    )(obj)


def sum_call(grad, ext, m, last, collective_id):
    full = ext.shape[1]
    t = full - 2 * m
    w = m if last else 2 * m
    side = t if last else full
    dma = pltpu.SemaphoreType.DMA
    return pl.pallas_call(
        functools.partial(sum_kernel_entry, m, last),
        out_shape=jax.ShapeDtypeStruct((2, side, side), jnp.float32),
        in_specs=[VM, VM],
        out_specs=VM,
        scratch_shapes=[
            pltpu.VMEM((2, full, full), jnp.float32),
            pltpu.VMEM((2, 2, m, full), jnp.float32),
            pltpu.VMEM((2, 2, t, w), jnp.float32),
            dma((2, 4)),
            dma((2, 4)),
            dma((2,)),
            dma((2,)),
            dma((2,)),
            dma((2,)),
        ],
        compiler_params=params(collective_id),
    )(grad, ext)


def sum_kernel_entry(m, last, grad_in, ext_ref, out_ref, work, *rest):
    def copy(row):
        work[:, pl.ds(row, 8), :] = grad_in[:, pl.ds(row, 8), :]

    by_rows(0, work.shape[1], copy)
    sum_kernel(m, last, work, ext_ref, out_ref, *rest)


def local(object_field, probe_field, measured, offsets, counts):
    side = probe_field.shape[1]
    m = side // 2
    fore, aft = tables(side)
    amps, starts = measured[0, 0], jnp.swapaxes(offsets[0, 0], 0, 1)
    ext = halo_call(object_field, m)
    for iteration in range(ITERS):
        last = iteration + 1 == ITERS
        grad = window_call(ext, probe_field, amps, fore, aft, starts, counts)
        ext = sum_call(grad, ext, m, last, 1 + iteration)
    return ext


def solution(mesh):
    return jax.shard_map(
        local,
        mesh=mesh,
        in_specs=(
            P(None, "gy", "gx"),
            P(),
            P("gy", "gx", None, None, None),
            P("gy", "gx", None, None),
            P("gy", "gx"),
        ),
        out_specs=P(None, "gy", "gx"),
        check_vma=False,
    )
```
